512 devices in a mesh: dp: 32 (over x, z), seq: 16 (over y, core).
Axes of the slice: x: 4, y: 8, z: 8, core: 2. Of those that a mesh axis runs over, the one named last changes fastest.
Arguments:
- queries: bfloat16 [65536, 1024], P(('dp', 'seq')), parts along dimension 0, may hold values from -6 to 6
- keyvals: bfloat16 [524288, 8, 128], P(('dp', 'seq')), parts along dimension 0, may hold values from -16 to 16
- residual: bfloat16 [65536, 1024], P(('dp', 'seq')), parts along dimension 0, may hold values from -16 to 16
- out_weight: bfloat16 [1024, 1024], P('seq'), may hold values from -0.1875 to 0.1875
- norm_gain: float32 [1024], replicated, may hold values from 0.25 to 1.75
- expert_up: bfloat16 [16, 1024, 512], P('seq'), may hold values from -0.1875 to 0.1875
- expert_down: bfloat16 [16, 256, 1024], P('seq'), may hold values from -0.375 to 0.375
- expert_ids: int32 [65536, 8], P(('dp', 'seq')), parts along dimension 0, may hold values from 0 to 15, as said below
- slot_index: int32 [65536, 8], P(('dp', 'seq')), parts along dimension 0, may hold values from 0 to 79, as said below
- gate_weights: float32 [65536, 8], P(('dp', 'seq')), parts along dimension 0, may hold values from 0.05 to 0.5
Outputs:
- layer_out: bfloat16 [65536, 1024], P(('dp', 'seq')), parts along dimension 0
The draws below stay inside these ranges and needn't reach their ends.
There are 32 independent parts, one for each index of `dp`. The reference program is written for one: setup_inputs(seed, part) draws one part's arguments, and reference() takes and returns one part's arrays. A program takes and returns all parts, laid end to end along the dimension named above; an argument that names none is the same for every part. Nothing has to cross between parts.
Inputs may be any that keep to these rules, and one draw needn't show every extreme that they name: `expert_ids`: each row names 8 different experts. Among the 128 rows of one device no expert is named by more than 80 rows, and in every draw one expert is named by exactly 80 rows on every device. `slot_index`: rows of one device that name the same expert have different slots.
All inputs are finite; a program needn't handle non-finite values.
Results may differ from the reference program's by a relative error of at most 0.014.
Values may be sent and summed in bfloat16 or wider, within the bound.
A program may use at most 64 MiB of HBM per device.

```python
import math
import jax
import jax.numpy as jnp
from jax import lax

D = 1024
HEADS = 16
KVH = 8
HEAD = 64
EXPERTS = 16
TOP = 8
FF = 256
SEQ_DEV = 1024
QROWS = 128
LEN = 16384
QTOK = 2048
CAP = 80
N_SEQ = 16


def route_tables(key):
    groups = QTOK // QROWS
    spread_key, label_key, order_key = jax.random.split(key, 3)
    spare = QROWS * TOP - CAP
    base_load = spare // (EXPERTS - 1)
    surplus = spare % (EXPERTS - 1)
    reach = min(CAP - base_load - 1, base_load - 1)
    paired = (EXPERTS - 1) // 2
    shifts = jax.random.randint(spread_key, (groups, paired), 0, reach + 1).astype(jnp.int32)
    others = base_load + (jnp.arange(EXPERTS - 1) < surplus).astype(jnp.int32)
    moved = jnp.zeros((groups, EXPERTS - 1), jnp.int32)
    moved = moved.at[:, 0:2 * paired:2].set(shifts)
    moved = moved.at[:, 1:2 * paired:2].set(-shifts)
    counts = jnp.concatenate([jnp.full((groups, 1), CAP, jnp.int32), others[None, :] + moved], axis=1)
    ends = jnp.cumsum(counts, axis=1)
    begins = ends - counts
    places = jnp.arange(QROWS * TOP).astype(jnp.int32)
    owner = jnp.sum((places[None, :, None] >= ends[:, None, :]).astype(jnp.int32), axis=2).astype(jnp.int32)
    slot_of = places[None, :] - jnp.take_along_axis(begins, owner, axis=1)
    owner = owner.reshape(groups, TOP, QROWS).transpose(0, 2, 1)
    slot_of = slot_of.reshape(groups, TOP, QROWS).transpose(0, 2, 1)
    orders = jax.vmap(lambda one_key: jax.random.permutation(one_key, QROWS))(jax.random.split(order_key, groups))
    owner = jnp.take_along_axis(owner, orders[:, :, None], axis=1)
    slot_of = jnp.take_along_axis(slot_of, orders[:, :, None], axis=1)
    labels = jax.random.permutation(label_key, EXPERTS).astype(jnp.int32)
    chosen = labels[owner]
    return (chosen.reshape(QTOK, TOP).astype(jnp.int32), slot_of.reshape(QTOK, TOP).astype(jnp.int32))


def draw_expert_ids(key, part):
    tables = route_tables(key)
    return tables[0]


def draw_slot_index(key, part):
    tables = route_tables(key)
    return tables[1]


def draw_queries(key, part):
    key = jax.random.fold_in(key, 5)
    groups = QTOK // QROWS
    values = jax.random.truncated_normal(key, -4.0, 4.0, (groups, QROWS, HEADS, HEAD), jnp.float32)
    return values.reshape(QTOK, HEADS * HEAD).astype(jnp.bfloat16)


def draw_keyvals(key, part):
    key = jax.random.fold_in(key, 7)
    base_key, scale_key = jax.random.split(key, 2)
    values = jax.random.truncated_normal(base_key, -4.0, 4.0, (LEN, KVH, 2 * HEAD), jnp.float32)
    row_scale = jnp.exp(jax.random.uniform(scale_key, (LEN, 1, 1), jnp.float32, math.log(1.8), math.log(2.2)))
    keys = values[..., :HEAD] * row_scale
    carried = values[..., HEAD:] * 2.0
    return jnp.concatenate([keys, carried], axis=-1).astype(jnp.bfloat16)


def draw_residual(key, part):
    key = jax.random.fold_in(key, 9)
    base_key, row_key, column_key = jax.random.split(key, 3)
    row_scale = jnp.exp(jax.random.uniform(row_key, (QTOK, 1), jnp.float32, math.log(0.1), math.log(1.0)))
    column_scale = jnp.exp(jax.random.uniform(column_key, (1, D), jnp.float32, math.log(0.3), math.log(3.0)))
    values = jax.random.truncated_normal(base_key, -4.0, 4.0, (QTOK, D), jnp.float32)
    return (values * row_scale * column_scale).astype(jnp.bfloat16)


def block_levels(own_key, extent, shards, smallest, top_value):
    def one(dim, parts):
        draws = jax.random.uniform(jax.random.fold_in(jax.random.fold_in(own_key, 6), dim), (parts,), jnp.float32, smallest / len(shards), top_value / len(shards))
        return jnp.repeat(jnp.exp(draws), extent[dim] // parts).reshape((-1,) + (1,) * (len(extent) - dim - 1))

    level = one(*shards[0])
    for cut in shards[1:]:
        level = level * one(*cut)
    return level


def normal_values(key, extent, scale, most, shards=(), dtype=jnp.bfloat16):
    entries = jax.random.normal(key, extent, jnp.float32) * scale
    if len(shards) > 0:
        entries = block_levels(key, extent, shards, -0.22, 0.18) * entries
    return jnp.clip(entries, min=-most, max=most).astype(dtype)


def setup_inputs(seed: int = 0, part: int = 0) -> dict:
    seeds = jax.random.split(jax.random.key(seed), 11)
    own_keys = jax.random.split(jax.random.fold_in(seeds[10], part), 11)
    return {
        "queries": draw_queries(jax.random.fold_in(jax.random.fold_in(seeds[10], part), 71), part),
        "keyvals": draw_keyvals(jax.random.fold_in(jax.random.fold_in(seeds[10], part), 71), part),
        "residual": draw_residual(jax.random.fold_in(jax.random.fold_in(seeds[10], part), 71), part),
        "out_weight": normal_values(seeds[3], (HEADS * HEAD, D), (HEADS * HEAD) ** -0.5, 0.1875, ((0, 16),)),
        "norm_gain": jnp.clip(1.0 + 0.15 * jax.random.normal(seeds[4], (D,), jnp.float32), 0.25, 1.75),
        "expert_up": normal_values(seeds[5], (EXPERTS, D, 2 * FF), D ** -0.5, 0.1875, ((0, 16),)),
        "expert_down": normal_values(seeds[6], (EXPERTS, FF, D), FF ** -0.5, 0.375, ((0, 16),)),
        "expert_ids": draw_expert_ids(jax.random.fold_in(jax.random.fold_in(seeds[10], part), 71), part),
        "slot_index": draw_slot_index(jax.random.fold_in(jax.random.fold_in(seeds[10], part), 71), part),
        "gate_weights": jnp.clip(jnp.exp(math.log(0.5) - 2.3025851 * jax.random.uniform(own_keys[9], (QTOK, TOP), jnp.float32) ** block_levels(own_keys[9], (QTOK, TOP), ((0, 16),), -0.2, 0.2)), 0.05, 0.5),
    }


MASKED = -1e+30

def reference(queries, keyvals, residual, out_weight, norm_gain, expert_up, expert_down, expert_ids, slot_index, gate_weights):
    query_count = QROWS * N_SEQ
    length = SEQ_DEV * N_SEQ
    score_scale = HEAD ** (-0.5)
    row_ids = jnp.arange(query_count)
    query_pos = row_ids // QROWS * SEQ_DEV + row_ids % QROWS
    key_pos = jnp.arange(length)
    visible = key_pos[None, :] <= query_pos[:, None]
    grouped = queries.reshape(query_count, KVH, 2, HEAD).transpose(1, 2, 0, 3)
    per_group = keyvals.transpose(1, 0, 2)

    def one_group(inputs):
        query_pair, key_values = inputs
        scores = jnp.einsum('gqd,kd->gqk', query_pair.astype(jnp.float32), key_values[:, :HEAD].astype(jnp.float32)) * score_scale
        scores = jnp.where(visible[None], scores, MASKED)
        highest = lax.optimization_barrier(jnp.max(scores, axis=-1, keepdims=True))
        weights = jnp.exp(scores - highest)
        totals = lax.optimization_barrier(jnp.sum(weights, axis=-1, keepdims=True))
        rounded = lax.optimization_barrier(weights.astype(jnp.bfloat16))
        summed = jnp.einsum('gqk,kd->gqd', rounded.astype(jnp.float32), key_values[:, HEAD:].astype(jnp.float32))
        return (summed / totals).astype(jnp.bfloat16)
    context = lax.map(one_group, (grouped, per_group))
    context = context.transpose(2, 0, 1, 3).reshape(query_count, HEADS * HEAD)
    hidden = (residual.astype(jnp.float32) + jnp.dot(context, out_weight, preferred_element_type=jnp.float32)).astype(jnp.bfloat16)
    widened = lax.optimization_barrier(hidden).astype(jnp.float32)
    normed = (widened * lax.rsqrt(lax.optimization_barrier(jnp.mean(widened * widened, axis=-1, keepdims=True)) + 1e-05) * norm_gain).astype(jnp.bfloat16)
    normed = lax.optimization_barrier(normed)
    source = (row_ids // QROWS).astype(jnp.int32)
    target = expert_ids * CAP + slot_index
    buffers = jnp.zeros((N_SEQ, EXPERTS * CAP, D), jnp.bfloat16)
    buffers = buffers.at[source[:, None], target].set(jnp.broadcast_to(normed[:, None, :], (query_count, TOP, D)))
    experts_in = buffers.reshape(N_SEQ, EXPERTS, CAP, D).transpose(1, 0, 2, 3).reshape(EXPERTS, N_SEQ * CAP, D)
    projected = jnp.einsum('erd,edf->erf', experts_in.astype(jnp.float32), expert_up.astype(jnp.float32))
    activated = (jax.nn.silu(projected[..., :FF]) * projected[..., FF:]).astype(jnp.bfloat16)
    activated = lax.optimization_barrier(activated)
    produced = jnp.einsum('erf,efd->erd', activated.astype(jnp.float32), expert_down.astype(jnp.float32)).astype(jnp.bfloat16)
    produced = lax.optimization_barrier(produced.reshape(EXPERTS, N_SEQ, CAP, D))
    picked = produced[expert_ids, source[:, None], slot_index]
    mixture = lax.optimization_barrier(jnp.sum(gate_weights[..., None] * picked.astype(jnp.float32), axis=1))
    return (widened + mixture).astype(jnp.bfloat16)
```

```python
import functools

import jax
import jax.numpy as jnp
from jax import lax
from jax.experimental import pallas as pl
from jax.experimental.pallas import tpu as pltpu
from jax.sharding import PartitionSpec as P

CHIPS = 8
ROWS = 128
KEYS = 1024
HEAD = 64
FF = 256
LOW = -1e30
MESH = pl.DeviceIdType.MESH
OFFSETS = (1, 7, 2, 6, 3, 5, 4)


def send(src, dst, send_sem, recv_sem, **where):
    return pltpu.make_async_remote_copy(
        src_ref=src,
        dst_ref=dst,
        send_sem=send_sem,
        recv_sem=recv_sem,
        device_id=where,
        device_id_type=MESH,
    )


def chip_columns(chip):
    return pl.ds(pl.multiple_of(chip * 128, 128), 128)


def attend_kernel(
    kv, q, out,
    kvland, qland, qpad, vt, acc, top, mland, cbuf, cland,
    own_sem, kv_s, kv_r, q_s, q_r, f_s, f_r, m_s, m_r, c_s, c_r,
):
    s = lax.axis_index("seq")
    c = s // 2
    k = lax.rem(s, 2)
    sib = s + 1 - 2 * k

    def chip(d):
        return lax.rem(c + d, CHIPS)

    def peer(d):
        return chip(d) * 2 + k

    barrier = pltpu.get_barrier_semaphore()
    for d in OFFSETS:
        pl.semaphore_signal(barrier, inc=1, device_id={"seq": peer(d)}, device_id_type=MESH)
    pl.semaphore_signal(barrier, inc=1, device_id={"seq": sib}, device_id_type=MESH)
    own_kv = pltpu.make_async_copy(kv.at[c], kvland.at[0], own_sem)
    own_kv.start()
    qland[s] = q[:, chip_columns(c)]
    pl.semaphore_wait(barrier, CHIPS)

    q_out = {d: send(q.at[:, chip_columns(chip(d))], qland.at[s], q_s.at[d], q_r.at[d], seq=peer(d)) for d in OFFSETS}
    kv_out = {d: send(kv.at[chip(d)], kvland.at[d], kv_s.at[d], kv_r.at[d], seq=peer(d)) for d in OFFSETS}
    for d in OFFSETS:
        q_out[d].start()
    q_on = {0: send(qland.at[s], qland.at[s], f_s.at[0], f_r.at[0], seq=sib)}
    q_on[0].start()
    for d in OFFSETS:
        kv_out[d].start()

    acc[...] = jnp.zeros_like(acc)
    top[...] = jnp.full_like(top, LOW)
    vt[HEAD:, :] = jnp.ones((16, KEYS), jnp.bfloat16)

    for d in OFFSETS:
        q_out[d].wait_recv()
        t = peer(CHIPS - d)
        q_on[d] = send(qland.at[t], qland.at[t], f_s.at[d], f_r.at[d], seq=sib)
        q_on[d].start()
    for d in (0,) + OFFSETS:
        q_on[d].wait_recv()

    def prepare(t, carry):
        x = qland[t].astype(jnp.float32) * (HEAD**-0.5)
        first = lax.broadcasted_iota(jnp.int32, (ROWS, 128), 1) < HEAD
        qpad[t, 0:ROWS, :] = jnp.where(first, x, 0.0).astype(jnp.bfloat16)
        qpad[t, ROWS:, :] = jnp.where(first, pltpu.roll(x, HEAD, 1), 0.0).astype(jnp.bfloat16)
        return carry

    lax.fori_loop(0, 2 * CHIPS, prepare, 0)

    def fold(i, scores, values, mask=None):
        if mask is not None:
            scores = jnp.where(mask, scores, LOW)
        old = top[i]
        new = jnp.maximum(old, jnp.max(scores, axis=0, keepdims=True))
        probs = jnp.exp(scores - new)
        if mask is not None:
            probs = jnp.where(mask, probs, 0.0)
        acc[i] = acc[i] * jnp.exp(old - new) + jnp.dot(
            values, probs.astype(jnp.bfloat16), preferred_element_type=jnp.float32
        )
        top[i] = new

    def place(t):
        return lax.rem(t, 2) * CHIPS + t // 2

    def score(keys, t):
        return lax.dot_general(keys, qpad[t], (((1,), (1,)), ((), ())), preferred_element_type=jnp.float32)

    def process(d):
        source = peer(CHIPS - d) if d else s
        for r in range(0, KEYS, 128):
            block = jnp.transpose(kvland[d, r : r + 128, :].astype(jnp.float32))
            vt[0:HEAD, r : r + 128] = block[HEAD:, :].astype(jnp.bfloat16)
        key_row = lax.broadcasted_iota(jnp.int32, (ROWS, 2 * ROWS), 0)
        query_row = lax.rem(lax.broadcasted_iota(jnp.int32, (ROWS, 2 * ROWS), 1), ROWS)
        fold(place(source), score(kvland[d, 0:ROWS, :], source), vt[:, 0:ROWS], key_row <= query_row)

        def step(t, carry):
            fold(place(t), score(kvland[d], t), vt[...])
            return carry

        lax.fori_loop(source + 1, 2 * CHIPS, step, 0)

    own_kv.wait()
    process(0)
    for d in OFFSETS:
        kv_out[d].wait_recv()
        process(d)

    def note(i, carry):
        acc[i, 72:80, :] = jnp.broadcast_to(top[i], (8, 2 * ROWS))
        return carry

    lax.fori_loop(0, 2 * CHIPS, note, 0)
    halves = pl.ds(pl.multiple_of((1 - k) * CHIPS, CHIPS), CHIPS)
    swap = send(acc.at[halves], mland, m_s, m_r, seq=sib)
    swap.start()
    swap.wait_recv()

    def finish(i):
        mine, theirs = acc[k * CHIPS + i], mland[i]
        ma, mb = mine[72:73], theirs[72:73]
        both = jnp.maximum(ma, mb)
        wa, wb = jnp.exp(ma - both), jnp.exp(mb - both)
        merged = mine * wa + theirs * wb
        ctx = merged[0:HEAD] / merged[HEAD : HEAD + 1]
        ctx = jnp.concatenate([ctx[:, 0:ROWS], ctx[:, ROWS:]], axis=0)
        return jnp.transpose(ctx).astype(jnp.bfloat16)

    c_out = {}
    for d in OFFSETS:
        cbuf[d] = finish(chip(d))
        c_out[d] = send(cbuf.at[d], cland.at[:, chip_columns(c)], c_s.at[d], c_r.at[d], seq=peer(d))
        c_out[d].start()
    cland[:, chip_columns(c)] = finish(c)
    for d in OFFSETS:
        c_out[d].wait_recv()
    out[...] = cland[...]
    for d in OFFSETS:
        q_out[d].wait_send()
        kv_out[d].wait_send()
        q_on[d].wait_send()
        c_out[d].wait_send()
    q_on[0].wait_send()
    swap.wait_send()


def attend(kv, q):
    dma = pltpu.SemaphoreType.DMA
    vmem = pl.BlockSpec(memory_space=pltpu.VMEM)
    return pl.pallas_call(
        attend_kernel,
        out_shape=jax.ShapeDtypeStruct((ROWS, 1024), jnp.bfloat16),
        in_specs=[vmem, vmem],
        out_specs=vmem,
        scratch_shapes=[
            pltpu.VMEM((CHIPS, KEYS, 128), jnp.bfloat16),
            pltpu.VMEM((2 * CHIPS, ROWS, 128), jnp.bfloat16),
            pltpu.VMEM((2 * CHIPS, 2 * ROWS, 128), jnp.bfloat16),
            pltpu.VMEM((HEAD + 16, KEYS), jnp.bfloat16),
            pltpu.VMEM((2 * CHIPS, HEAD + 16, 2 * ROWS), jnp.float32),
            pltpu.VMEM((2 * CHIPS, 1, 2 * ROWS), jnp.float32),
            pltpu.VMEM((CHIPS, HEAD + 16, 2 * ROWS), jnp.float32),
            pltpu.VMEM((CHIPS, ROWS, 128), jnp.bfloat16),
            pltpu.VMEM((ROWS, 1024), jnp.bfloat16),
            dma, dma((CHIPS,)), dma((CHIPS,)), dma((CHIPS,)), dma((CHIPS,)), dma((CHIPS,)), dma((CHIPS,)),
            dma, dma, dma((CHIPS,)), dma((CHIPS,)),
        ],
        compiler_params=pltpu.CompilerParams(
            collective_id=0, has_side_effects=True, vmem_limit_bytes=32 * 1024 * 1024
        ),
        cost_estimate=pl.CostEstimate(flops=60_000_000_000, bytes_accessed=100_000_000, transcendentals=16_000_000),
    )(kv, q)


def experts_kernel(ctx, residual, proj, gain, gates, sib_gates, up, down, out, xboth, ysib, yland, x_s, x_r, y_s, y_r):
    s = lax.axis_index("seq")
    k = lax.rem(s, 2)
    sib = s + 1 - 2 * k
    barrier = pltpu.get_barrier_semaphore()
    pl.semaphore_signal(barrier, inc=1, device_id={"seq": sib}, device_id_type=MESH)
    hidden = (
        residual[...].astype(jnp.float32) + jnp.dot(ctx[...], proj[...], preferred_element_type=jnp.float32)
    ).astype(jnp.bfloat16)
    wide = hidden.astype(jnp.float32)
    normed = wide * lax.rsqrt(jnp.mean(wide * wide, axis=-1, keepdims=True) + 1e-05) * gain[...]
    xboth[0:ROWS, :] = normed.astype(jnp.bfloat16)
    pl.semaphore_wait(barrier, 1)
    swap = send(xboth.at[pl.ds(0, ROWS)], xboth.at[pl.ds(ROWS, ROWS)], x_s, x_r, seq=sib)
    swap.start()
    swap.wait()
    x = xboth[...]
    weights = jnp.concatenate([gates[...], sib_gates[...]], axis=0)
    column = lax.broadcasted_iota(jnp.int32, weights.shape, 1)
    total = jnp.zeros((2 * ROWS, 1024), jnp.float32)
    for j in range(CHIPS):
        projected = jnp.dot(x, up[:, j].reshape(1024, 512), preferred_element_type=jnp.float32)
        gate, lift = projected[:, :FF], projected[:, FF:]
        scale = jnp.sum(jnp.where(column == 2 * j + k, weights, 0.0), axis=1, keepdims=True)
        act = (gate / (1.0 + jnp.exp(-gate)) * lift * scale).astype(jnp.bfloat16)
        low = down[0:16, j].reshape(FF, 512)
        high = down[16:32, j].reshape(FF, 512)
        total = total + jnp.concatenate(
            [
                jnp.dot(act, low, preferred_element_type=jnp.float32),
                jnp.dot(act, high, preferred_element_type=jnp.float32),
            ],
            axis=1,
        )
    ysib[...] = total[ROWS:, :]
    back = send(ysib, yland, y_s, y_r, seq=sib)
    back.start()
    back.wait()
    out[...] = (wide + total[0:ROWS, :] + yland[...]).astype(jnp.bfloat16)


def experts(*args):
    dma = pltpu.SemaphoreType.DMA
    vmem = pl.BlockSpec(memory_space=pltpu.VMEM)
    return pl.pallas_call(
        experts_kernel,
        out_shape=jax.ShapeDtypeStruct((ROWS, 1024), jnp.bfloat16),
        in_specs=[vmem] * 8,
        out_specs=vmem,
        scratch_shapes=[
            pltpu.VMEM((2 * ROWS, 1024), jnp.bfloat16),
            pltpu.VMEM((ROWS, 1024), jnp.float32),
            pltpu.VMEM((ROWS, 1024), jnp.float32),
            dma, dma, dma, dma,
        ],
        compiler_params=pltpu.CompilerParams(
            collective_id=1, has_side_effects=True, vmem_limit_bytes=40 * 1024 * 1024
        ),
    )(*args)


def body(
    queries, keyvals, residual, out_weight, norm_gain, expert_up, expert_down, expert_ids, slot_index, gate_weights
):
    dp = lax.axis_index("dp")
    core = lax.rem(lax.axis_index("seq"), 2)
    up_part = lax.dynamic_slice(expert_up[0], (dp * 32, 0), (32, 512))
    down_part = lax.dynamic_slice(expert_down[0], (dp % 16 * 16, dp // 16 * 512), (16, 512))
    part = jnp.concatenate([up_part, down_part], axis=0)
    column = lax.all_gather(part, "seq", axis=0).reshape(CHIPS, 2, 48, 512)
    column = lax.dynamic_index_in_dim(column, core, 1, keepdims=False)
    whole = lax.all_gather(column, "dp", axis=0)
    proj = lax.all_gather(out_weight, "seq", axis=0, tiled=True)
    gates = jnp.sum(
        jnp.where(expert_ids[:, :, None] == jnp.arange(16), gate_weights[:, :, None], 0.0), axis=1
    )
    sib_gates = lax.ppermute(gates, "seq", [(i, i ^ 1) for i in range(16)])
    ctx = attend(keyvals.transpose(1, 0, 2), queries)
    return experts(
        ctx, residual, proj, norm_gain[None], gates, sib_gates, whole[:, :, :32], whole[:, :, 32:]
    )


def solution(mesh):
    rows = P(("dp", "seq"), None)
    placed = (
        rows,
        P(("dp", "seq"), None, None),
        rows,
        P("seq", None),
        P(),
        P("seq", None, None),
        P("seq", None, None),
        rows,
        rows,
        rows,
    )
    return jax.shard_map(body, mesh=mesh, in_specs=placed, out_specs=rows, check_vma=False)
```

```python
import jax
import jax.numpy as jnp
from jax import lax
from jax.experimental import pallas as pl
from jax.experimental.pallas import tpu as pltpu
from jax.sharding import PartitionSpec as P

CHIPS = 8
XS = 4
ZS = 8
ROWS = 128
KEYS = 1024
HEAD = 64
FF = 256
SLOTS = 10
LOW = -1e30
MESH = pl.DeviceIdType.MESH
OFFSETS = (1, 7, 2, 6, 3, 5, 4)
TRANSFERS = 128


def chip_columns(chip):
    return pl.ds(pl.multiple_of(chip * 128, 128), 128)


def rows_at(start, size):
    return pl.ds(pl.multiple_of(start, size), size)


def layer_kernel(
    kv, q, residual, proj, gain, own_up, own_down, ids, chosen, out,
    kvland, qland, qt, vt, acc, top, sa, sb, pa, pb, aa, ab, mland, cbuf, cland,
    ups, downs, weight, gates, x, hid, total, yland, own_sem, snd, rcv,
):
    f32, bf16 = jnp.float32, jnp.bfloat16
    s = lax.axis_index("seq")
    c = s // 2
    k = lax.rem(s, 2)
    sib = s + 1 - 2 * k
    dp = lax.axis_index("dp")
    px = dp // ZS
    pz = lax.rem(dp, ZS)

    def chip(d):
        return lax.rem(c + d + CHIPS, CHIPS)

    def peer(d):
        return chip(d) * 2 + k

    def xat(i):
        return lax.rem(px + i + XS, XS)

    def zat(i):
        return lax.rem(pz + i + ZS, ZS)

    def plane(i, j):
        return xat(i) * ZS + zat(j)

    sent = []

    def transfer(src, dst, **where):
        n = len(sent)
        copy = pltpu.make_async_remote_copy(
            src_ref=src, dst_ref=dst, send_sem=snd.at[n], recv_sem=rcv.at[n], device_id=where, device_id_type=MESH
        )
        sent.append(copy)
        return copy

    def begin(*copies):
        for copy in copies:
            copy.start()

    def arrive(*copies):
        for copy in copies:
            copy.wait_recv()

    barrier = pltpu.get_barrier_semaphore()
    others = [{"seq": peer(d)} for d in OFFSETS] + [{"seq": sib}]
    others += [{"dp": plane(i, 0)} for i in (1, 2, 3)] + [{"dp": plane(0, j)} for j in (1, -1)]
    for where in others:
        pl.semaphore_signal(barrier, inc=1, device_id=where, device_id_type=MESH)
    own_kv = pltpu.make_async_copy(kv.at[c], kvland.at[0], own_sem)
    own_kv.start()
    qland[s] = q[:, chip_columns(c)]
    lane = lax.broadcasted_iota(jnp.int32, (ROWS, 128), 1)
    mine = jnp.zeros((ROWS, 128), f32)
    for j in range(ids.shape[1]):
        mine = mine + jnp.where(lane == ids[:, j : j + 1], chosen[:, j : j + 1], 0.0)
    gates[0:ROWS, :] = mine
    downs[pz, px, 7 + c // 4, :, chip_columns(lax.rem(c, 4))] = proj[rows_at(px * 16, 16), chip_columns(pz)]
    pl.semaphore_wait(barrier, len(others))

    quarter = pz * XS + px
    first = []
    for d in OFFSETS:
        slot = CHIPS - d - 1
        first.append(transfer(own_up.at[0, rows_at(dp * 32, 32)], ups.at[dp, slot], seq=peer(d)))
        first.append(
            transfer(
                own_down.at[0, rows_at(lax.rem(quarter, 16) * 16, 16), pl.ds(pl.multiple_of(quarter // 16 * 512, 512), 512)],
                downs.at[pz, px, slot],
                seq=peer(d),
            )
        )
        first.append(
            transfer(
                proj.at[rows_at(px * 16, 16), chip_columns(pz)],
                downs.at[pz, px, 7 + c // 4, :, chip_columns(lax.rem(c, 4))],
                seq=peer(d),
            )
        )
    begin(*first)

    q_out = {d: transfer(q.at[:, chip_columns(chip(d))], qland.at[s], seq=peer(d)) for d in OFFSETS}
    kv_out = {d: transfer(kv.at[chip(d)], kvland.at[d], seq=peer(d)) for d in OFFSETS}
    q_on = {d: transfer(qland.at[peer(-d)], qland.at[peer(-d)], seq=sib) for d in (0,) + OFFSETS}
    gate_on = transfer(gates.at[pl.ds(0, ROWS)], gates.at[pl.ds(ROWS, ROWS)], seq=sib)
    begin(*q_out.values())
    begin(q_on[0], gate_on)
    begin(*kv_out.values())

    def up_to(i, j, **where):
        return transfer(ups.at[plane(i, j)], ups.at[plane(i, j)], **where)

    def down_to(j, part=None, **where):
        ref = downs.at[zat(j)] if part is None else downs.at[zat(j), pl.ds(part, 2)]
        return transfer(ref, ref, **where)

    right, left = {"dp": plane(1, 0)}, {"dp": plane(-1, 0)}
    upward, downward = {"dp": plane(0, 1)}, {"dp": plane(0, -1)}
    zp = {i: up_to(0, 1 - i, **upward) for i in (1, 2, 3, 4)}
    zm = {i: up_to(0, i - 1, **downward) for i in (1, 2, 3)}
    around = (0, 1, -1, 2, -2, 3, -3, 4)
    xp = {o: up_to(0, o, **right) for o in around}
    xm = {o: up_to(0, o, **left) for o in around}
    xf = {o: up_to(-1, o, **right) for o in (0, 1, 2, 3)}
    xf.update({o: up_to(1, o, **left) for o in (-1, -2, -3, 4)})
    bx = [transfer(downs.at[pz, px], downs.at[pz, px], dp=plane(i, 0)) for i in (1, -1, 2)]
    bp = {i: down_to(1 - i, **upward) for i in (1, 2, 3)}
    bm = {i: down_to(i - 1, **downward) for i in (1, 2, 3)}
    bp[4] = down_to(-3, 0, **upward)
    bm[4] = down_to(3, 2, **downward)

    def w1():
        arrive(*first)
        begin(zp[1], zm[1], xp[0], xm[0], *bx)

    def w2():
        arrive(zp[1], zm[1])
        begin(zp[2], zm[2], xp[-1], xm[-1], xp[1], xm[1])

    def w3():
        arrive(*bx)
        begin(bp[1], bm[1])

    def w4():
        arrive(zp[2], zm[2])
        begin(zp[3], zm[3], xp[-2], xm[-2], xp[2], xm[2])

    def w5():
        arrive(xp[0])
        begin(xf[0])

    def w6():
        arrive(zp[3], zm[3])
        begin(zp[4], xp[-3], xm[-3], xp[3], xm[3])

    def w7():
        arrive(bp[1], bm[1])
        begin(bp[2], bm[2])

    def w8():
        arrive(zp[4])
        begin(xp[4], xm[4])

    def w9():
        arrive(xp[1], xm[-1])
        begin(xf[1], xf[-1])

    def w10():
        arrive(bp[2], bm[2])
        begin(bp[3], bm[3])

    def w11():
        arrive(xp[2], xm[-2])
        begin(xf[2], xf[-2])

    def w12():
        arrive(xp[3], xm[-3])
        begin(xf[3], xf[-3])

    def w13():
        arrive(bp[3], bm[3])
        begin(bp[4], bm[4])

    def w14():
        arrive(xm[4])
        begin(xf[4])

    def w15():
        arrive(xm[0], xm[1], xp[-1], xm[2], xp[-2], xm[3], xp[-3], xp[4])
        arrive(*xf.values())
        arrive(bp[4], bm[4])

    acc[...] = jnp.zeros_like(acc)
    top[...] = jnp.full_like(top, LOW)
    vt[HEAD:, :] = jnp.ones((16, KEYS), bf16)
    qt[...] = jnp.zeros_like(qt)

    for d in OFFSETS:
        arrive(q_out[d])
        begin(q_on[d])
    w1()
    arrive(*q_on.values())

    def prepare(t, carry):
        y = jnp.transpose(qland[t].astype(f32) * (HEAD**-0.5)).astype(bf16)
        qt[t, 0:HEAD, 0:ROWS] = y[0:HEAD]
        qt[t, 0:HEAD, ROWS:] = y[HEAD:]
        return carry

    lax.fori_loop(0, 2 * CHIPS, prepare, 0)

    def place(t):
        return lax.rem(t, 2) * SLOTS + t // 2

    def process(d):
        source = peer(-d)
        for r in range(0, KEYS, 128):
            block = jnp.transpose(kvland[d, r : r + 128, :].astype(f32))
            vt[0:HEAD, r : r + 128] = block[HEAD:, :].astype(bf16)

        scores = jnp.dot(kvland[d, 0:ROWS, :], qt[source], preferred_element_type=f32)
        key_row = lax.broadcasted_iota(jnp.int32, (ROWS, 2 * ROWS), 0)
        query_row = lax.rem(lax.broadcasted_iota(jnp.int32, (ROWS, 2 * ROWS), 1), ROWS)
        scores = jnp.where(key_row <= query_row, scores, LOW)
        i = place(source)
        old = top[i]
        new = jnp.maximum(old, jnp.max(scores, axis=0, keepdims=True))
        probs = jnp.where(key_row <= query_row, jnp.exp(scores - new), 0.0).astype(bf16)
        acc[i] = acc[i] * jnp.exp(old - new) + jnp.dot(vt[:, 0:ROWS], probs, preferred_element_type=f32)
        top[i] = new

        def score(n, scores):
            scores[...] = jnp.dot(kvland[d], qt[source + 1 + n], preferred_element_type=f32)

        def soften(n, scores, probs, shrink):
            i = place(source + 1 + n)
            old = top[i]
            new = jnp.maximum(old, jnp.max(scores[...], axis=0, keepdims=True))
            probs[...] = jnp.exp(scores[...] - new).astype(bf16)
            shrink[...] = jnp.exp(old - new)
            top[i] = new

        def add(n, probs, shrink):
            i = place(source + 1 + n)
            acc[i] = acc[i] * shrink[...] + jnp.dot(vt[...], probs[...], preferred_element_type=f32)

        score(0, sa)
        soften(0, sa, pa, aa)
        score(1, sb)

        def step(m, carry):
            n = 2 * m
            score(n + 2, sa)
            soften(n + 1, sb, pb, ab)
            add(n, pa, aa)
            score(n + 3, sb)
            soften(n + 2, sa, pa, aa)
            add(n + 1, pb, ab)
            return carry

        lax.fori_loop(0, (2 * CHIPS - source) // 2, step, 0)

    own_kv.wait()
    process(0)
    for d, services in zip(
        OFFSETS, ((w2, w3, w5), (w4,), (w6, w7), (w8, w9), (w10, w11), (w12,), (w13, w14))
    ):
        for service in services:
            service()
        arrive(kv_out[d])
        process(d)

    def note(i, carry):
        acc[i, 72:80, :] = jnp.broadcast_to(top[i], (8, 2 * ROWS))
        return carry

    lax.fori_loop(0, 2 * SLOTS, note, 0)
    swap = transfer(acc.at[pl.ds((1 - k) * SLOTS, CHIPS)], mland, seq=sib)
    begin(swap)
    arrive(swap)

    def finish(i):
        mine, theirs = acc[k * SLOTS + i], mland[i]
        ma, mb = mine[72:73], theirs[72:73]
        both = jnp.maximum(ma, mb)
        merged = mine * jnp.exp(ma - both) + theirs * jnp.exp(mb - both)
        ctx = merged[0:HEAD] / merged[HEAD : HEAD + 1]
        ctx = jnp.concatenate([ctx[:, 0:ROWS], ctx[:, ROWS:]], axis=0)
        return jnp.transpose(ctx).astype(bf16)

    c_out = {d: transfer(cbuf.at[d], cland.at[:, chip_columns(c)], seq=peer(d)) for d in OFFSETS}
    for d in OFFSETS:
        cbuf[d] = finish(chip(d))
        begin(c_out[d])
    cland[:, chip_columns(c)] = finish(c)
    w15()

    for i in range(CHIPS):
        for j in range(ZS):
            block = downs[j, :, 7 + i // 4, :, 128 * (i % 4) : 128 * (i % 4) + 128]
            weight[i, k, :, 128 * j : 128 * j + 128] = block.reshape(HEAD, 128)
    w_on = transfer(weight.at[:, k], weight.at[:, k], seq=sib)
    begin(w_on)
    arrive(w_on)
    arrive(*c_out.values())

    hidden = (
        residual[...].astype(f32)
        + jnp.dot(cland[...], weight[...].reshape(1024, 1024), preferred_element_type=f32)
    ).astype(bf16)
    hid[...] = hidden
    wide = hidden.astype(f32)
    normed = wide * lax.rsqrt(jnp.mean(wide * wide, axis=-1, keepdims=True) + 1e-05) * gain[...]
    x[0:ROWS, :] = normed.astype(bf16)
    x_on = transfer(x.at[pl.ds(0, ROWS)], x.at[pl.ds(ROWS, ROWS)], seq=sib)
    begin(x_on)
    arrive(x_on, gate_on)

    def expert(e, up, low, high):
        projected = jnp.dot(x[...], up, preferred_element_type=f32)
        gate, lift = projected[:, :FF], projected[:, FF:]
        column = lax.broadcasted_iota(jnp.int32, (2 * ROWS, 128), 1)
        scale = jnp.sum(jnp.where(column == e, gates[...], 0.0), axis=1, keepdims=True)
        act = (gate / (1.0 + jnp.exp(-gate)) * lift * scale).astype(bf16)
        return (
            jnp.dot(act, low, preferred_element_type=f32),
            jnp.dot(act, high, preferred_element_type=f32),
        )

    low, high = expert(s, own_up[0], own_down[0, :, 0:512], own_down[0, :, 512:])
    total[:, 0:512] = low
    total[:, 512:] = high

    def other(j, carry):
        low, high = expert(
            chip(j + 1) * 2 + k,
            ups[:, j].reshape(1024, 512),
            downs[0:4, :, j].reshape(FF, 512),
            downs[4:8, :, j].reshape(FF, 512),
        )
        total[:, 0:512] += low
        total[:, 512:] += high
        return carry

    lax.fori_loop(0, CHIPS - 1, other, 0)
    y_on = transfer(total.at[pl.ds(ROWS, ROWS)], yland, seq=sib)
    begin(y_on)
    arrive(y_on)
    out[...] = (hid[...].astype(f32) + total[0:ROWS, :] + yland[...]).astype(bf16)
    for copy in sent:
        copy.wait_send()


def body(
    queries, keyvals, residual, out_weight, norm_gain, expert_up, expert_down, expert_ids, slot_index, gate_weights
):
    dma = pltpu.SemaphoreType.DMA
    vmem = pl.BlockSpec(memory_space=pltpu.VMEM)
    f32, bf16 = jnp.float32, jnp.bfloat16
    return pl.pallas_call(
        layer_kernel,
        out_shape=jax.ShapeDtypeStruct((ROWS, 1024), bf16),
        in_specs=[vmem] * 9,
        out_specs=vmem,
        scratch_shapes=[
            pltpu.VMEM((CHIPS, KEYS, 128), bf16),
            pltpu.VMEM((2 * CHIPS, ROWS, 128), bf16),
            pltpu.VMEM((2 * SLOTS, 128, 2 * ROWS), bf16),
            pltpu.VMEM((HEAD + 16, KEYS), bf16),
            pltpu.VMEM((2 * SLOTS, HEAD + 16, 2 * ROWS), f32),
            pltpu.VMEM((2 * SLOTS, 1, 2 * ROWS), f32),
            pltpu.VMEM((KEYS, 2 * ROWS), f32),
            pltpu.VMEM((KEYS, 2 * ROWS), f32),
            pltpu.VMEM((KEYS, 2 * ROWS), bf16),
            pltpu.VMEM((KEYS, 2 * ROWS), bf16),
            pltpu.VMEM((1, 2 * ROWS), f32),
            pltpu.VMEM((1, 2 * ROWS), f32),
            pltpu.VMEM((CHIPS, HEAD + 16, 2 * ROWS), f32),
            pltpu.VMEM((CHIPS, ROWS, 128), bf16),
            pltpu.VMEM((ROWS, 1024), bf16),
            pltpu.VMEM((XS * ZS, CHIPS - 1, 32, 512), bf16),
            pltpu.VMEM((ZS, XS, CHIPS + 1, 16, 512), bf16),
            pltpu.VMEM((CHIPS, 2, HEAD, 1024), bf16),
            pltpu.VMEM((2 * ROWS, 128), f32),
            pltpu.VMEM((2 * ROWS, 1024), bf16),
            pltpu.VMEM((ROWS, 1024), bf16),
            pltpu.VMEM((2 * ROWS, 1024), f32),
            pltpu.VMEM((ROWS, 1024), f32),
            dma,
            dma((TRANSFERS,)),
            dma((TRANSFERS,)),
        ],
        compiler_params=pltpu.CompilerParams(
            collective_id=0, has_side_effects=True, vmem_limit_bytes=56 * 1024 * 1024
        ),
        cost_estimate=pl.CostEstimate(flops=60_000_000_000, bytes_accessed=100_000_000, transcendentals=16_000_000),
    )(
        keyvals.transpose(1, 0, 2), queries, residual, out_weight, norm_gain[None], expert_up, expert_down,
        expert_ids, gate_weights,
    )


def solution(mesh):
    rows = P(("dp", "seq"), None)
    placed = (
        rows,
        P(("dp", "seq"), None, None),
        rows,
        P("seq", None),
        P(),
        P("seq", None, None),
        P("seq", None, None),
        rows,
        rows,
        rows,
    )
    return jax.shard_map(body, mesh=mesh, in_specs=placed, out_specs=rows, check_vma=False)
```

```python
import jax
import jax.numpy as jnp
from jax import lax
from jax.experimental import pallas as pl
from jax.experimental.pallas import tpu as pltpu
from jax.sharding import PartitionSpec as P

CHIPS = 8
XS = 4
ZS = 8
ROWS = 128
KEYS = 1024
HEAD = 64
FF = 256
LOW = -1e30
MESH = pl.DeviceIdType.MESH
OFFSETS = (1, 7, 2, 6, 3, 5, 4)
TRANSFERS = 128


def chip_columns(chip):
    return pl.ds(pl.multiple_of(chip * 128, 128), 128)


def rows_at(start, size):
    return pl.ds(pl.multiple_of(start, size), size)


def layer_kernel(
    kv, q, residual, proj, gain, up_in, down_in, ids, chosen, out,
    kvland, qland, qt, vt, acc, top, sa, sb, pa, pb, aa, ab, cbuf, cland,
    own_up, own_down, ups, downs, projs, weight, gates, x, hid, total, yland, own_sem, up_sem, down_sem, snd, rcv,
):
    f32, bf16 = jnp.float32, jnp.bfloat16
    s = lax.axis_index("seq")
    c = s // 2
    k = lax.rem(s, 2)
    sib = s + 1 - 2 * k
    dp = lax.axis_index("dp")
    px = dp // ZS
    pz = lax.rem(dp, ZS)

    def chip(d):
        return lax.rem(c + d + CHIPS, CHIPS)

    def peer(d):
        return chip(d) * 2 + k

    def xat(i):
        return lax.rem(px + i + XS, XS)

    def zat(i):
        return lax.rem(pz + i + ZS, ZS)

    def plane(i, j):
        return xat(i) * ZS + zat(j)

    sent = []

    def transfer(src, dst, **where):
        n = len(sent)
        copy = pltpu.make_async_remote_copy(
            src_ref=src, dst_ref=dst, send_sem=snd.at[n], recv_sem=rcv.at[n], device_id=where, device_id_type=MESH
        )
        sent.append(copy)
        return copy

    def begin(*copies):
        for copy in copies:
            copy.start()

    def arrive(*copies):
        for copy in copies:
            copy.wait_recv()

    barrier = pltpu.get_barrier_semaphore()
    others = [{"seq": peer(d)} for d in OFFSETS] + [{"seq": sib}]
    others += [{"dp": plane(i, 0)} for i in (1, 2, 3)] + [{"dp": plane(0, j)} for j in (1, -1)]
    for where in others:
        pl.semaphore_signal(barrier, inc=1, device_id=where, device_id_type=MESH)
    own_kv = pltpu.make_async_copy(kv.at[c], kvland.at[0, 0], own_sem)
    own_kv.start()
    up_copy = pltpu.make_async_copy(up_in.at[0], own_up, up_sem)
    up_copy.start()
    down_copy = pltpu.make_async_copy(down_in.at[0], own_down, down_sem)
    down_copy.start()
    qland[c] = q[:, chip_columns(c)]
    expert_row = lax.broadcasted_iota(jnp.int32, (128, ROWS), 0)
    mine = jnp.zeros((128, ROWS), f32)
    for j in range(ids.shape[0]):
        mine = mine + jnp.where(expert_row == ids[j : j + 1, :], chosen[j : j + 1, :], 0.0)
    gates[0:ROWS, :] = jnp.transpose(mine)
    projs[pz, px, c // 4, :, chip_columns(lax.rem(c, 4))] = proj[rows_at(px * 16, 16), chip_columns(pz)]
    pl.semaphore_wait(barrier, len(others))

    quarter = pz * XS + px
    first = [
        transfer(up_in.at[0, rows_at(dp * 32, 32)], ups.at[dp, CHIPS - d - 1], seq=peer(d)) for d in OFFSETS
    ]
    second = []
    for d in OFFSETS:
        second.append(
            transfer(
                proj.at[rows_at(px * 16, 16), chip_columns(pz)],
                projs.at[pz, px, c // 4, :, chip_columns(lax.rem(c, 4))],
                seq=peer(d),
            )
        )
        part = pl.ds(pl.multiple_of(quarter // 16 * 512, 512), 512)
        second.append(
            transfer(
                down_in.at[0, rows_at(lax.rem(quarter, 16) * 16, 16), part],
                downs.at[pz, px, CHIPS - d - 1],
                seq=peer(d),
            )
        )
    begin(*first, *second)

    q_out = {d: transfer(q.at[:, chip_columns(chip(d))], qland.at[c], seq=peer(d)) for d in OFFSETS}
    kv_out = {d: transfer(kv.at[chip(d)], kvland.at[0, d], seq=peer(d)) for d in OFFSETS}
    kv_on = {d: transfer(kvland.at[0, d], kvland.at[1, d], seq=sib) for d in (0,) + OFFSETS}
    gate_on = transfer(gates.at[pl.ds(0, ROWS)], gates.at[pl.ds(ROWS, ROWS)], seq=sib)
    begin(*q_out.values())
    begin(*[kv_out[d] for d in OFFSETS[:4]])
    own_kv.wait()
    begin(kv_on[0], gate_on)

    def up_to(i, j, **where):
        return transfer(ups.at[plane(i, j)], ups.at[plane(i, j)], **where)

    def row_to(rows, j, part=None, **where):
        ref = rows.at[zat(j)] if part is None else rows.at[zat(j), pl.ds(part, 2)]
        return transfer(ref, ref, **where)

    right, left = {"dp": plane(1, 0)}, {"dp": plane(-1, 0)}
    upward, downward = {"dp": plane(0, 1)}, {"dp": plane(0, -1)}
    zp = {i: up_to(0, 1 - i, **upward) for i in (1, 2, 3, 4)}
    zm = {i: up_to(0, i - 1, **downward) for i in (1, 2, 3)}
    around = (0, 1, -1, 2, -2, 3, -3, 4)
    xp = {o: up_to(0, o, **right) for o in around}
    xm = {o: up_to(0, o, **left) for o in around}
    xf = {o: up_to(-1, o, **right) for o in (0, 1, 2, 3)}
    xf.update({o: up_to(1, o, **left) for o in (-1, -2, -3, 4)})

    def rows_about(rows):
        along = [transfer(rows.at[pz, px], rows.at[pz, px], dp=plane(i, 0)) for i in (1, -1, 2)]
        plus = {i: row_to(rows, 1 - i, **upward) for i in (1, 2, 3)}
        minus = {i: row_to(rows, i - 1, **downward) for i in (1, 2, 3)}
        plus[4] = row_to(rows, -3, 0, **upward)
        minus[4] = row_to(rows, 3, 2, **downward)
        return along, plus, minus

    ox, op, om = rows_about(projs)
    bx, bp, bm = rows_about(downs)

    def w1():
        arrive(*first)
        begin(zp[1], zm[1], xp[0], xm[0])
        arrive(*second)
        begin(*ox, *bx)

    def w2():
        arrive(zp[1], zm[1])
        begin(zp[2], zm[2], xp[-1], xm[-1], xp[1], xm[1])

    def w3():
        arrive(*ox)
        begin(op[1], om[1])
        arrive(*bx)
        begin(bp[1], bm[1])

    def w4():
        arrive(zp[2], zm[2])
        arrive(op[1], om[1])
        begin(op[2], om[2])
        begin(zp[3], zm[3], xp[-2], xm[-2], xp[2], xm[2])

    def w5():
        arrive(xp[0])
        begin(xf[0])

    def w6():
        arrive(zp[3], zm[3])
        arrive(op[2], om[2])
        begin(op[3], om[3])
        begin(zp[4], xp[-3], xm[-3], xp[3], xm[3])

    def w7():
        arrive(bp[1], bm[1])
        begin(bp[2], bm[2])

    def w8():
        arrive(zp[4])
        begin(xp[4], xm[4])
        arrive(op[3], om[3])
        begin(op[4], om[4])

    def w9():
        arrive(xp[1], xm[-1])
        begin(xf[1], xf[-1])

    def w10():
        arrive(bp[2], bm[2])
        begin(bp[3], bm[3])

    def w11():
        arrive(xp[2], xm[-2])
        begin(xf[2], xf[-2])

    def w12():
        arrive(xp[3], xm[-3])
        begin(xf[3], xf[-3])

    def w13():
        arrive(bp[3], bm[3])
        begin(bp[4], bm[4])

    def w14():
        arrive(xm[4])
        begin(xf[4])

    def w15():
        arrive(xm[0], xm[1], xp[-1], xm[2], xp[-2], xm[3], xp[-3], xp[4])
        arrive(*xf.values())
        arrive(bp[4], bm[4])

    acc[...] = jnp.zeros_like(acc)
    top[...] = jnp.full_like(top, LOW)
    vt[:, HEAD:, :] = jnp.ones((2, 16, KEYS), bf16)
    qt[...] = jnp.zeros_like(qt)

    w1()
    arrive(*q_out.values())

    def prepare(i, carry):
        y = jnp.transpose(qland[i].astype(f32) * (HEAD**-0.5)).astype(bf16)
        qt[i, 0:HEAD, 0:ROWS] = y[0:HEAD]
        qt[i, 0:HEAD, ROWS:] = y[HEAD:]
        return carry

    lax.fori_loop(0, CHIPS, prepare, 0)

    def process(d):
        near = chip(-d)
        for h in (0, 1):
            for r in range(0, KEYS, 128):
                block = jnp.transpose(kvland[h, d, r : r + 128, :].astype(f32))
                vt[h, 0:HEAD, r : r + 128] = block[HEAD:, :].astype(bf16)

        def shift(i, scores):
            old = top[i]
            new = jnp.maximum(old, jnp.max(scores, axis=0, keepdims=True))
            top[i] = new
            return new, jnp.exp(old - new)

        scores = jnp.dot(kvland[0, d, 0:ROWS, :], qt[near], preferred_element_type=f32)
        key_row = lax.broadcasted_iota(jnp.int32, (ROWS, 2 * ROWS), 0)
        query_row = lax.rem(lax.broadcasted_iota(jnp.int32, (ROWS, 2 * ROWS), 1), ROWS)
        scores = jnp.where(key_row <= query_row, scores, LOW)
        new, shrink = shift(near, scores)
        probs = jnp.where(key_row <= query_row, jnp.exp(scores - new), 0.0).astype(bf16)
        acc[near] = acc[near] * shrink + jnp.dot(vt[0, :, 0:ROWS], probs, preferred_element_type=f32)

        def before(m, carry):
            sa[...] = jnp.dot(kvland[1, d], qt[near], preferred_element_type=f32)
            new, shrink = shift(near, sa[...])
            pa[...] = jnp.exp(sa[...] - new).astype(bf16)
            acc[near] = acc[near] * shrink + jnp.dot(vt[1], pa[...], preferred_element_type=f32)
            return carry

        lax.fori_loop(0, k, before, 0)

        def score(i, h, scores):
            scores[...] = jnp.dot(kvland[h, d], qt[i], preferred_element_type=f32)

        def soften(i, scores, probs, shrink):
            new, shrink[...] = shift(i, scores[...])
            probs[...] = jnp.exp(scores[...] - new).astype(bf16)

        def add(i, h, probs, shrink):
            acc[i] = acc[i] * shrink[...] + jnp.dot(vt[h], probs[...], preferred_element_type=f32)

        score(near + 1, 0, sa)
        soften(near + 1, sa, pa, aa)
        score(near + 1, 1, sb)

        def step(m, carry):
            i = near + 1 + m
            score(i + 1, 0, sa)
            soften(i, sb, pb, ab)
            add(i, 0, pa, aa)
            score(i + 1, 1, sb)
            soften(i + 1, sa, pa, aa)
            add(i, 1, pb, ab)
            return carry

        lax.fori_loop(0, CHIPS - 1 - near, step, 0)

    def pass_on(d):
        arrive(kv_out[d])
        begin(kv_on[d])

    def fold(d):
        arrive(kv_on[d])
        process(d)

    fold(0)
    w2()
    pass_on(1)
    begin(kv_out[3], kv_out[5])
    w3()
    pass_on(7)
    fold(1)
    w5()
    w4()
    pass_on(2)
    begin(kv_out[4])
    fold(7)
    pass_on(6)
    fold(2)
    w6()
    fold(6)
    w7()
    w8()
    w9()
    pass_on(3)
    pass_on(5)
    fold(3)
    pass_on(4)
    fold(5)
    w10()
    w11()
    fold(4)
    w12()

    def finish(i):
        ctx = acc[i, 0:HEAD, :] / acc[i, HEAD : HEAD + 1, :]
        ctx = jnp.concatenate([ctx[:, 0:ROWS], ctx[:, ROWS:]], axis=0)
        return jnp.transpose(ctx).astype(bf16)

    c_out = {d: transfer(cbuf.at[d], cland.at[:, chip_columns(c)], seq=peer(d)) for d in OFFSETS}
    for d in OFFSETS:
        cbuf[d] = finish(chip(d))
        begin(c_out[d])
    cland[:, chip_columns(c)] = finish(c)

    arrive(op[4], om[4])
    for i in range(CHIPS):
        for j in range(ZS):
            block = projs[j, :, i // 4, :, 128 * (i % 4) : 128 * (i % 4) + 128]
            weight[i, k, :, 128 * j : 128 * j + 128] = block.reshape(HEAD, 128)
    w_on = transfer(weight.at[:, k], weight.at[:, k], seq=sib)
    begin(w_on)
    w13()
    arrive(w_on)
    arrive(*c_out.values())
    w14()

    hidden = (
        residual[...].astype(f32)
        + jnp.dot(cland[...], weight[...].reshape(1024, 1024), preferred_element_type=f32)
    ).astype(bf16)
    hid[...] = hidden
    wide = hidden.astype(f32)
    normed = wide * lax.rsqrt(jnp.mean(wide * wide, axis=-1, keepdims=True) + 1e-05) * gain[...]
    x[0:ROWS, :] = normed.astype(bf16)
    x_on = transfer(x.at[pl.ds(0, ROWS)], x.at[pl.ds(ROWS, ROWS)], seq=sib)
    begin(x_on)
    arrive(x_on, gate_on)
    w15()

    def expert(e, up, low, high):
        projected = jnp.dot(x[...], up, preferred_element_type=f32)
        gate, lift = projected[:, :FF], projected[:, FF:]
        column = lax.broadcasted_iota(jnp.int32, (2 * ROWS, 128), 1)
        scale = jnp.sum(jnp.where(column == e, gates[...], 0.0), axis=1, keepdims=True)
        act = (gate / (1.0 + jnp.exp(-gate)) * lift * scale).astype(bf16)
        return (
            jnp.dot(act, low, preferred_element_type=f32),
            jnp.dot(act, high, preferred_element_type=f32),
        )

    up_copy.wait()
    down_copy.wait()
    low, high = expert(s, own_up[...], own_down[:, 0:512], own_down[:, 512:])
    total[:, 0:512] = low
    total[:, 512:] = high

    def other(j, carry):
        low, high = expert(
            chip(j + 1) * 2 + k,
            ups[:, j].reshape(1024, 512),
            downs[0:4, :, j].reshape(FF, 512),
            downs[4:8, :, j].reshape(FF, 512),
        )
        total[:, 0:512] += low
        total[:, 512:] += high
        return carry

    lax.fori_loop(0, CHIPS - 1, other, 0)
    y_on = transfer(total.at[pl.ds(ROWS, ROWS)], yland, seq=sib)
    begin(y_on)
    arrive(y_on)
    out[...] = (hid[...].astype(f32) + total[0:ROWS, :] + yland[...]).astype(bf16)
    for copy in sent:
        copy.wait_send()


def body(
    queries, keyvals, residual, out_weight, norm_gain, expert_up, expert_down, expert_ids, slot_index, gate_weights
):
    dma = pltpu.SemaphoreType.DMA
    vmem = pl.BlockSpec(memory_space=pltpu.VMEM)
    hbm = pl.BlockSpec(memory_space=pl.ANY)
    f32, bf16 = jnp.float32, jnp.bfloat16
    return pl.pallas_call(
        layer_kernel,
        out_shape=jax.ShapeDtypeStruct((ROWS, 1024), bf16),
        in_specs=[hbm, vmem, vmem, vmem, vmem, hbm, hbm, vmem, vmem],
        out_specs=vmem,
        scratch_shapes=[
            pltpu.VMEM((2, CHIPS, KEYS, 128), bf16),
            pltpu.VMEM((CHIPS, ROWS, 128), bf16),
            pltpu.VMEM((CHIPS + 1, 128, 2 * ROWS), bf16),
            pltpu.VMEM((2, HEAD + 16, KEYS), bf16),
            pltpu.VMEM((CHIPS + 1, HEAD + 16, 2 * ROWS), f32),
            pltpu.VMEM((CHIPS + 1, 1, 2 * ROWS), f32),
            pltpu.VMEM((KEYS, 2 * ROWS), f32),
            pltpu.VMEM((KEYS, 2 * ROWS), f32),
            pltpu.VMEM((KEYS, 2 * ROWS), bf16),
            pltpu.VMEM((KEYS, 2 * ROWS), bf16),
            pltpu.VMEM((1, 2 * ROWS), f32),
            pltpu.VMEM((1, 2 * ROWS), f32),
            pltpu.VMEM((CHIPS, ROWS, 128), bf16),
            pltpu.VMEM((ROWS, 1024), bf16),
            pltpu.VMEM((1024, 512), bf16),
            pltpu.VMEM((FF, 1024), bf16),
            pltpu.VMEM((XS * ZS, CHIPS - 1, 32, 512), bf16),
            pltpu.VMEM((ZS, XS, CHIPS - 1, 16, 512), bf16),
            pltpu.VMEM((ZS, XS, 2, 16, 512), bf16),
            pltpu.VMEM((CHIPS, 2, HEAD, 1024), bf16),
            pltpu.VMEM((2 * ROWS, 128), f32),
            pltpu.VMEM((2 * ROWS, 1024), bf16),
            pltpu.VMEM((ROWS, 1024), bf16),
            pltpu.VMEM((2 * ROWS, 1024), f32),
            pltpu.VMEM((ROWS, 1024), f32),
            dma,
            dma,
            dma,
            dma((TRANSFERS,)),
            dma((TRANSFERS,)),
        ],
        compiler_params=pltpu.CompilerParams(
            collective_id=0, has_side_effects=True, vmem_limit_bytes=56 * 1024 * 1024
        ),
        cost_estimate=pl.CostEstimate(flops=60_000_000_000, bytes_accessed=100_000_000, transcendentals=16_000_000),
    )(
        keyvals.transpose(1, 0, 2), queries, residual, out_weight, norm_gain[None], expert_up, expert_down,
        expert_ids.T, gate_weights.T,
    )


def solution(mesh):
    rows = P(("dp", "seq"), None)
    placed = (
        rows,
        P(("dp", "seq"), None, None),
        rows,
        P("seq", None),
        P(),
        P("seq", None, None),
        P("seq", None, None),
        rows,
        rows,
        rows,
    )
    return jax.shard_map(body, mesh=mesh, in_specs=placed, out_specs=rows, check_vma=False)
```

```python
import jax
import jax.numpy as jnp
from jax import lax
from jax.experimental import pallas as pl
from jax.experimental.pallas import tpu as pltpu
from jax.sharding import PartitionSpec as P

CHIPS = 8
XS = 4
ZS = 8
ROWS = 128
KEYS = 1024
HEAD = 64
FF = 256
LOW = -1e30
MESH = pl.DeviceIdType.MESH
OFFSETS = (1, 7, 2, 6, 3, 5, 4)
TRANSFERS = 128


def chip_columns(chip):
    return pl.ds(pl.multiple_of(chip * 128, 128), 128)


def rows_at(start, size):
    return pl.ds(pl.multiple_of(start, size), size)


def layer_kernel(
    kv, q, residual, proj, gain, up_in, down_in, ids, chosen, out,
    kvland, qland, qt, vt, acc, top, sa, sb, pa, pb, aa, ab, cbuf, cland,
    own_up, own_down, ups, downs, projs, weight, gates, x, hid, total, yland, own_sem, up_sem, down_sem, snd, rcv,
):
    f32, bf16 = jnp.float32, jnp.bfloat16
    s = lax.axis_index("seq")
    c = s // 2
    k = lax.rem(s, 2)
    sib = s + 1 - 2 * k
    dp = lax.axis_index("dp")
    px = dp // ZS
    pz = lax.rem(dp, ZS)

    def chip(d):
        return lax.rem(c + d + CHIPS, CHIPS)

    def peer(d):
        return chip(d) * 2 + k

    def xat(i):
        return lax.rem(px + i + XS, XS)

    def zat(i):
        return lax.rem(pz + i + ZS, ZS)

    def plane(i, j):
        return xat(i) * ZS + zat(j)

    sent = []

    def transfer(src, dst, **where):
        n = len(sent)
        copy = pltpu.make_async_remote_copy(
            src_ref=src, dst_ref=dst, send_sem=snd.at[n], recv_sem=rcv.at[n], device_id=where, device_id_type=MESH
        )
        sent.append(copy)
        return copy

    def begin(*copies):
        for copy in copies:
            copy.start()

    def arrive(*copies):
        for copy in copies:
            copy.wait_recv()

    barrier = pltpu.get_barrier_semaphore()
    others = [{"seq": peer(d)} for d in OFFSETS] + [{"seq": sib}]
    others += [{"dp": plane(i, 0)} for i in (1, 2, 3)] + [{"dp": plane(0, j)} for j in (1, -1)]
    for where in others:
        pl.semaphore_signal(barrier, inc=1, device_id=where, device_id_type=MESH)
    own_kv = pltpu.make_async_copy(kv.at[c], kvland.at[0, 0], own_sem)
    own_kv.start()
    up_copy = pltpu.make_async_copy(up_in.at[0], own_up, up_sem)
    up_copy.start()
    down_copy = pltpu.make_async_copy(down_in.at[0], own_down, down_sem)
    down_copy.start()
    qland[c] = q[:, chip_columns(c)]
    expert_row = lax.broadcasted_iota(jnp.int32, (128, ROWS), 0)
    mine = jnp.zeros((128, ROWS), f32)
    for j in range(ids.shape[0]):
        mine = mine + jnp.where(expert_row == ids[j : j + 1, :], chosen[j : j + 1, :], 0.0)
    gates[0:ROWS, :] = jnp.transpose(mine)
    projs[pz, px, c // 4, :, chip_columns(lax.rem(c, 4))] = proj[rows_at(px * 16, 16), chip_columns(pz)]
    pl.semaphore_wait(barrier, len(others))

    quarter = pz * XS + px
    first = [
        transfer(up_in.at[0, rows_at(dp * 32, 32)], ups.at[dp, CHIPS - d - 1], seq=peer(d)) for d in OFFSETS
    ]
    second = []
    for d in OFFSETS:
        second.append(
            transfer(
                proj.at[rows_at(px * 16, 16), chip_columns(pz)],
                projs.at[pz, px, c // 4, :, chip_columns(lax.rem(c, 4))],
                seq=peer(d),
            )
        )
        part = pl.ds(pl.multiple_of(quarter // 16 * 512, 512), 512)
        second.append(
            transfer(
                down_in.at[0, rows_at(lax.rem(quarter, 16) * 16, 16), part],
                downs.at[pz, px, CHIPS - d - 1],
                seq=peer(d),
            )
        )
    begin(*first)

    q_out = {d: transfer(q.at[:, chip_columns(chip(d))], qland.at[c], seq=peer(d)) for d in OFFSETS}
    kv_out = {d: transfer(kv.at[chip(d)], kvland.at[0, d], seq=peer(d)) for d in OFFSETS}
    kv_on = {d: transfer(kvland.at[0, d], kvland.at[1, d], seq=sib) for d in (0,) + OFFSETS}
    gate_on = transfer(gates.at[pl.ds(0, ROWS)], gates.at[pl.ds(ROWS, ROWS)], seq=sib)
    begin(*q_out.values())
    begin(*second)
    own_kv.wait()
    begin(kv_on[0], gate_on)

    def up_to(i, j, **where):
        return transfer(ups.at[plane(i, j)], ups.at[plane(i, j)], **where)

    def row_to(rows, j, part=None, **where):
        ref = rows.at[zat(j)] if part is None else rows.at[zat(j), pl.ds(part, 2)]
        return transfer(ref, ref, **where)

    right, left = {"dp": plane(1, 0)}, {"dp": plane(-1, 0)}
    upward, downward = {"dp": plane(0, 1)}, {"dp": plane(0, -1)}
    zp = {i: up_to(0, 1 - i, **upward) for i in (1, 2, 3, 4)}
    zm = {i: up_to(0, i - 1, **downward) for i in (1, 2, 3)}
    around = (0, 1, -1, 2, -2, 3, -3, 4)
    xp = {o: up_to(0, o, **right) for o in around}
    xm = {o: up_to(0, o, **left) for o in around}
    xf = {o: up_to(-1, o, **right) for o in (0, 1, 2, 3)}
    xf.update({o: up_to(1, o, **left) for o in (-1, -2, -3, 4)})

    def rows_about(rows):
        along = [transfer(rows.at[pz, px], rows.at[pz, px], dp=plane(i, 0)) for i in (1, -1, 2)]
        plus = {i: row_to(rows, 1 - i, **upward) for i in (1, 2, 3)}
        minus = {i: row_to(rows, i - 1, **downward) for i in (1, 2, 3)}
        plus[4] = row_to(rows, -3, 0, **upward)
        minus[4] = row_to(rows, 3, 2, **downward)
        return along, plus, minus

    ox, op, om = rows_about(projs)
    bx, bp, bm = rows_about(downs)

    def w1():
        arrive(*first)
        begin(zp[1], zm[1], xp[0], xm[0])
        begin(*[kv_out[d] for d in OFFSETS[:4]])
        arrive(*second)
        begin(*ox, *bx)

    def w2():
        arrive(zp[1], zm[1])
        begin(zp[2], zm[2], xp[-1], xm[-1], xp[1], xm[1])

    def w3():
        arrive(*ox)
        begin(op[1], om[1])
        arrive(*bx)
        begin(bp[1], bm[1])

    def w4():
        arrive(zp[2], zm[2])
        arrive(op[1], om[1])
        begin(op[2], om[2])
        begin(zp[3], zm[3], xp[-2], xm[-2], xp[2], xm[2])

    def w5():
        arrive(xp[0])
        begin(xf[0])

    def w6():
        arrive(zp[3], zm[3])
        arrive(op[2], om[2])
        begin(op[3], om[3])
        begin(zp[4], xp[-3], xm[-3], xp[3], xm[3])

    def w7():
        arrive(bp[1], bm[1])
        begin(bp[2], bm[2])

    def w8():
        arrive(zp[4])
        begin(xp[4], xm[4])
        arrive(op[3], om[3])
        begin(op[4], om[4])

    def w9():
        arrive(xp[1], xm[-1])
        begin(xf[1], xf[-1])

    def w10():
        arrive(bp[2], bm[2])
        begin(bp[3], bm[3])

    def w11():
        arrive(xp[2], xm[-2])
        begin(xf[2], xf[-2])

    def w12():
        arrive(xp[3], xm[-3])
        begin(xf[3], xf[-3])

    def w13():
        arrive(bp[3], bm[3])
        begin(bp[4], bm[4])

    def w14():
        arrive(xm[4])
        begin(xf[4])

    def w15():
        arrive(xm[0], xm[1], xp[-1], xm[2], xp[-2], xm[3], xp[-3], xp[4])
        arrive(*xf.values())
        arrive(bp[4], bm[4])

    acc[...] = jnp.zeros_like(acc)
    top[...] = jnp.full_like(top, LOW)
    vt[:, HEAD:, :] = jnp.ones((2, 16, KEYS), bf16)
    qt[...] = jnp.zeros_like(qt)

    w1()
    arrive(*q_out.values())

    def prepare(i, carry):
        y = jnp.transpose(qland[i].astype(f32) * (HEAD**-0.5)).astype(bf16)
        qt[i, 0:HEAD, 0:ROWS] = y[0:HEAD]
        qt[i, 0:HEAD, ROWS:] = y[HEAD:]
        return carry

    lax.fori_loop(0, CHIPS, prepare, 0)

    def process(d):
        near = chip(-d)
        for h in (0, 1):
            for r in range(0, KEYS, 128):
                block = jnp.transpose(kvland[h, d, r : r + 128, :].astype(f32))
                vt[h, 0:HEAD, r : r + 128] = block[HEAD:, :].astype(bf16)

        def shift(i, scores):
            old = top[i]
            new = jnp.maximum(old, jnp.max(scores, axis=0, keepdims=True))
            top[i] = new
            return new, jnp.exp(old - new)

        scores = jnp.dot(kvland[0, d, 0:ROWS, :], qt[near], preferred_element_type=f32)
        key_row = lax.broadcasted_iota(jnp.int32, (ROWS, 2 * ROWS), 0)
        query_row = lax.rem(lax.broadcasted_iota(jnp.int32, (ROWS, 2 * ROWS), 1), ROWS)
        scores = jnp.where(key_row <= query_row, scores, LOW)
        new, shrink = shift(near, scores)
        probs = jnp.where(key_row <= query_row, jnp.exp(scores - new), 0.0).astype(bf16)
        acc[near] = acc[near] * shrink + jnp.dot(vt[0, :, 0:ROWS], probs, preferred_element_type=f32)

        def before(m, carry):
            sa[...] = jnp.dot(kvland[1, d], qt[near], preferred_element_type=f32)
            new, shrink = shift(near, sa[...])
            pa[...] = jnp.exp(sa[...] - new).astype(bf16)
            acc[near] = acc[near] * shrink + jnp.dot(vt[1], pa[...], preferred_element_type=f32)
            return carry

        lax.fori_loop(0, k, before, 0)

        def score(i, h, scores):
            scores[...] = jnp.dot(kvland[h, d], qt[i], preferred_element_type=f32)

        def soften(i, scores, probs, shrink):
            new, shrink[...] = shift(i, scores[...])
            probs[...] = jnp.exp(scores[...] - new).astype(bf16)

        def add(i, h, probs, shrink):
            acc[i] = acc[i] * shrink[...] + jnp.dot(vt[h], probs[...], preferred_element_type=f32)

        score(near + 1, 0, sa)
        soften(near + 1, sa, pa, aa)
        score(near + 1, 1, sb)

        def step(m, carry):
            i = near + 1 + m
            score(i + 1, 0, sa)
            soften(i, sb, pb, ab)
            add(i, 0, pa, aa)
            score(i + 1, 1, sb)
            soften(i + 1, sa, pa, aa)
            add(i, 1, pb, ab)
            return carry

        lax.fori_loop(0, CHIPS - 1 - near, step, 0)

    def pass_on(d):
        arrive(kv_out[d])
        begin(kv_on[d])

    def fold(d):
        arrive(kv_on[d])
        process(d)

    fold(0)
    w2()
    pass_on(1)
    begin(kv_out[3], kv_out[5])
    w3()
    pass_on(7)
    fold(1)
    w5()
    w4()
    pass_on(2)
    begin(kv_out[4])
    fold(7)
    pass_on(6)
    fold(2)
    w6()
    fold(6)
    w7()
    w8()
    w9()
    pass_on(3)
    pass_on(5)
    fold(3)
    pass_on(4)
    w10()
    fold(5)
    w11()
    fold(4)
    w12()

    def finish(i):
        ctx = acc[i, 0:HEAD, :] / acc[i, HEAD : HEAD + 1, :]
        ctx = jnp.concatenate([ctx[:, 0:ROWS], ctx[:, ROWS:]], axis=0)
        return jnp.transpose(ctx).astype(bf16)

    c_out = {d: transfer(cbuf.at[d], cland.at[:, chip_columns(c)], seq=peer(d)) for d in OFFSETS}
    for d in OFFSETS:
        cbuf[d] = finish(chip(d))
        begin(c_out[d])
    cland[:, chip_columns(c)] = finish(c)

    arrive(op[4], om[4])
    for i in range(CHIPS):
        for j in range(ZS):
            block = projs[j, :, i // 4, :, 128 * (i % 4) : 128 * (i % 4) + 128]
            weight[i, k, :, 128 * j : 128 * j + 128] = block.reshape(HEAD, 128)
    w_on = transfer(weight.at[:, k], weight.at[:, k], seq=sib)
    begin(w_on)
    w13()
    arrive(w_on)
    arrive(*c_out.values())
    w14()

    hidden = (
        residual[...].astype(f32)
        + jnp.dot(cland[...], weight[...].reshape(1024, 1024), preferred_element_type=f32)
    ).astype(bf16)
    hid[...] = hidden
    wide = hidden.astype(f32)
    normed = wide * lax.rsqrt(jnp.mean(wide * wide, axis=-1, keepdims=True) + 1e-05) * gain[...]
    x[0:ROWS, :] = normed.astype(bf16)
    x_on = transfer(x.at[pl.ds(0, ROWS)], x.at[pl.ds(ROWS, ROWS)], seq=sib)
    begin(x_on)
    arrive(x_on, gate_on)

    def expert(e, up, low, high):
        projected = jnp.dot(x[...], up, preferred_element_type=f32)
        gate, lift = projected[:, :FF], projected[:, FF:]
        column = lax.broadcasted_iota(jnp.int32, (2 * ROWS, 128), 1)
        scale = jnp.sum(jnp.where(column == e, gates[...], 0.0), axis=1, keepdims=True)
        act = (gate / (1.0 + jnp.exp(-gate)) * lift * scale).astype(bf16)
        return (
            jnp.dot(act, low, preferred_element_type=f32),
            jnp.dot(act, high, preferred_element_type=f32),
        )

    up_copy.wait()
    down_copy.wait()
    low, high = expert(s, own_up[...], own_down[:, 0:512], own_down[:, 512:])
    total[:, 0:512] = low
    total[:, 512:] = high
    w15()

    def other(j, carry):
        low, high = expert(
            chip(j + 1) * 2 + k,
            ups[:, j].reshape(1024, 512),
            downs[0:4, :, j].reshape(FF, 512),
            downs[4:8, :, j].reshape(FF, 512),
        )
        total[:, 0:512] += low
        total[:, 512:] += high
        return carry

    lax.fori_loop(0, CHIPS - 1, other, 0)
    y_on = transfer(total.at[pl.ds(ROWS, ROWS)], yland, seq=sib)
    begin(y_on)
    arrive(y_on)
    out[...] = (hid[...].astype(f32) + total[0:ROWS, :] + yland[...]).astype(bf16)
    for copy in sent:
        copy.wait_send()


def body(
    queries, keyvals, residual, out_weight, norm_gain, expert_up, expert_down, expert_ids, slot_index, gate_weights
):
    dma = pltpu.SemaphoreType.DMA
    vmem = pl.BlockSpec(memory_space=pltpu.VMEM)
    hbm = pl.BlockSpec(memory_space=pl.ANY)
    f32, bf16 = jnp.float32, jnp.bfloat16
    return pl.pallas_call(
        layer_kernel,
        out_shape=jax.ShapeDtypeStruct((ROWS, 1024), bf16),
        in_specs=[hbm, vmem, vmem, vmem, vmem, hbm, hbm, vmem, vmem],
        out_specs=vmem,
        scratch_shapes=[
            pltpu.VMEM((2, CHIPS, KEYS, 128), bf16),
            pltpu.VMEM((CHIPS, ROWS, 128), bf16),
            pltpu.VMEM((CHIPS + 1, 128, 2 * ROWS), bf16),
            pltpu.VMEM((2, HEAD + 16, KEYS), bf16),
            pltpu.VMEM((CHIPS + 1, HEAD + 16, 2 * ROWS), f32),
            pltpu.VMEM((CHIPS + 1, 1, 2 * ROWS), f32),
            pltpu.VMEM((KEYS, 2 * ROWS), f32),
            pltpu.VMEM((KEYS, 2 * ROWS), f32),
            pltpu.VMEM((KEYS, 2 * ROWS), bf16),
            pltpu.VMEM((KEYS, 2 * ROWS), bf16),
            pltpu.VMEM((1, 2 * ROWS), f32),
            pltpu.VMEM((1, 2 * ROWS), f32),
            pltpu.VMEM((CHIPS, ROWS, 128), bf16),
            pltpu.VMEM((ROWS, 1024), bf16),
            pltpu.VMEM((1024, 512), bf16),
            pltpu.VMEM((FF, 1024), bf16),
            pltpu.VMEM((XS * ZS, CHIPS - 1, 32, 512), bf16),
            pltpu.VMEM((ZS, XS, CHIPS - 1, 16, 512), bf16),
            pltpu.VMEM((ZS, XS, 2, 16, 512), bf16),
            pltpu.VMEM((CHIPS, 2, HEAD, 1024), bf16),
            pltpu.VMEM((2 * ROWS, 128), f32),
            pltpu.VMEM((2 * ROWS, 1024), bf16),
            pltpu.VMEM((ROWS, 1024), bf16),
            pltpu.VMEM((2 * ROWS, 1024), f32),
            pltpu.VMEM((ROWS, 1024), f32),
            dma,
            dma,
            dma,
            dma((TRANSFERS,)),
            dma((TRANSFERS,)),
        ],
        compiler_params=pltpu.CompilerParams(
            collective_id=0, has_side_effects=True, vmem_limit_bytes=56 * 1024 * 1024
        ),
        cost_estimate=pl.CostEstimate(flops=60_000_000_000, bytes_accessed=100_000_000, transcendentals=16_000_000),
    )(
        keyvals.transpose(1, 0, 2), queries, residual, out_weight, norm_gain[None], expert_up, expert_down,
        expert_ids.T, gate_weights.T,
    )


def solution(mesh):
    rows = P(("dp", "seq"), None)
    placed = (
        rows,
        P(("dp", "seq"), None, None),
        rows,
        P("seq", None),
        P(),
        P("seq", None, None),
        P("seq", None, None),
        rows,
        rows,
        rows,
    )
    return jax.shard_map(body, mesh=mesh, in_specs=placed, out_specs=rows, check_vma=False)
```
